32 devices in a mesh: parts: 2 (over x), slab: 16 (over z, y, core).
Axes of the slice: x: 2, y: 2, z: 4, core: 2. Of those that a mesh axis runs over, the one named last changes fastest.
Arguments:
- volume: bfloat16 [32, 16, 64, 256], P(('parts', 'slab')), parts along dimension 0, may hold values from -6 to 6
- plane_weight: bfloat16 [2, 5, 5, 16, 256], replicated, may hold values from -0.3125 to 0.3125
- norm_gain: bfloat16 [2, 256], replicated, may hold values from 0.099609375 to 1.8984375
- expand_weight: bfloat16 [2, 256, 1024], replicated, may hold values from -0.375 to 0.375
- down_weight: bfloat16 [2, 1024, 256], replicated, may hold values from -0.1875 to 0.1875
- depth_weight: bfloat16 [2, 3, 256], replicated, may hold values from -3 to 3
Outputs:
- features: bfloat16 [32, 16, 64, 256], P(('parts', 'slab')), parts along dimension 0
The draws below stay inside these ranges and needn't reach their ends.
There are 2 independent parts, one for each index of `parts`. The reference program is written for one: setup_inputs(seed, part) draws one part's arguments, and reference() takes and returns one part's arrays. A program takes and returns all parts, laid end to end along the dimension named above; an argument that names none is the same for every part. Nothing has to cross between parts.
All inputs are finite; a program needn't handle non-finite values.
Results may differ from the reference program's by a relative error of at most 0.01.
Values may be sent and summed in bfloat16 or wider, within the bound.
A program may use at most 64 MiB of HBM per device.

```python
import jax
import jax.numpy as jnp
from jax import lax

C = 256
HID = 1024
GROUP = 16
XW = 16
YW = 64
LAYERS = 2
FIRST_DILATION = 1
SECOND_DILATION = 4
Z = 16


def levels(key, dims, pieces, low, largest):
    level, own = 1.0, jax.random.fold_in(key, 6)
    for dim, parts in pieces:
        heights = jnp.exp(jax.random.uniform(jax.random.fold_in(own, dim), (parts,), jnp.float32, low / len(pieces), largest / len(pieces)))
        level = level * jnp.repeat(heights, dims[dim] // parts).reshape([-1 if axis == dim else 1 for axis in range(len(dims))])
    return level


def gaussian(key, extent, width, reach, cuts=(), held_as=jnp.bfloat16):
    loudness = levels(key, extent, cuts, -0.22, 0.18) if cuts else 1.0
    array = jax.random.normal(key, extent, jnp.float32) * width * loudness
    return jnp.minimum(jnp.maximum(array, -reach), reach).astype(held_as)


def setup_inputs(seed: int = 0, part: int = 0) -> dict:
    arg_keys = jax.random.split(jax.random.key(seed), 7)
    own_keys = jax.random.split(jax.random.fold_in(arg_keys[6], part), 7)
    volume = gaussian(own_keys[0], (Z, XW, YW, C), 1.0, 6.0, ((0, 16),))
    plane_weight = gaussian(arg_keys[1], (LAYERS, 5, 5, GROUP, C), (25 * GROUP) ** -0.5, 0.3125)
    norm_gain = jnp.clip(1.0 + 0.18 * jax.random.normal(arg_keys[2], (LAYERS, C), jnp.float32), 0.099609375, 1.8984375).astype(jnp.bfloat16)
    expand_weight = gaussian(arg_keys[3], (LAYERS, C, HID), C ** -0.5, 0.375)
    down_weight = gaussian(arg_keys[4], (LAYERS, HID, C), HID ** -0.5, 0.1875)
    depth_weight = gaussian(arg_keys[5], (LAYERS, 3, C), 0.6, 3.0)
    return dict(volume=volume, plane_weight=plane_weight, norm_gain=norm_gain, expand_weight=expand_weight, down_weight=down_weight, depth_weight=depth_weight)


epsilon = 1e-06

def plane_mix(plane_slice, weight, gain, up_matrix, down_matrix):
    extent_x, extent_y, channels = plane_slice.shape
    group_size = weight.shape[2]
    group_count = channels // group_size
    padded = jnp.pad(plane_slice.astype(jnp.float32), ((2, 2), (2, 2), (0, 0)))
    accumulated = jnp.zeros((extent_x, extent_y, group_count, group_size), jnp.float32)
    for offset_row in range(5):
        for offset_col in range(5):
            window = padded[offset_row:offset_row + extent_x, offset_col:offset_col + extent_y]
            window = window.reshape(extent_x, extent_y, group_count, group_size)
            kernel = weight[offset_row, offset_col].astype(jnp.float32).reshape(group_size, group_count, group_size)
            accumulated = accumulated + jnp.einsum('xyni,inj->xynj', window, kernel)
    conv_out = accumulated.reshape(extent_x, extent_y, channels)
    scale_inv = lax.rsqrt(lax.optimization_barrier(jnp.mean(conv_out * conv_out, axis=-1, keepdims=True)) + epsilon)
    normed = (conv_out * scale_inv * gain.astype(jnp.float32)).astype(jnp.bfloat16)
    hidden = jax.nn.silu(jnp.dot(normed.reshape(-1, channels), up_matrix, preferred_element_type=jnp.float32)).astype(jnp.bfloat16)
    mixed = jnp.dot(hidden, down_matrix, preferred_element_type=jnp.float32).astype(jnp.bfloat16)
    return mixed.reshape(extent_x, extent_y, channels)

def reference(volume, plane_weight, norm_gain, expand_weight, down_weight, depth_weight):
    current = volume
    for layer_number, dilation_factor in enumerate((FIRST_DILATION, SECOND_DILATION)):

        def slice_wise(plane_slice):
            return plane_mix(plane_slice, plane_weight[layer_number], norm_gain[layer_number], expand_weight[layer_number], down_weight[layer_number])
        mixed = lax.map(slice_wise, current)
        coeffs = depth_weight[layer_number].astype(jnp.float32)
        mixed_wide = mixed.astype(jnp.float32)
        total_slices = mixed.shape[0]
        padded = jnp.pad(mixed_wide, ((dilation_factor, dilation_factor), (0, 0), (0, 0), (0, 0)))
        depth_term = coeffs[0] * padded[:total_slices] + coeffs[1] * mixed_wide + coeffs[2] * padded[2 * dilation_factor:]
        depth_term = depth_term.astype(jnp.bfloat16)
        current = (current.astype(jnp.float32) + depth_term.astype(jnp.float32)).astype(jnp.bfloat16)
    return current
```

```python
import functools

import jax
import jax.numpy as jnp
from jax import lax
from jax.experimental import pallas as pl
from jax.experimental.pallas import tpu as pltpu
from jax.sharding import PartitionSpec as P

DILATIONS = (1, 4)
TAPS = 5
EPSILON = 1e-06
CHUNK_X = 4


def kernel(devices, extent_x, extent_y, vol_hbm, plane_hbm, gain_ref, expand_hbm, down_hbm, depth_ref, out_hbm,
           cur, plane, expand, down, mask, taps, window, mixed, lower, upper, result,
           load_sem, send_sem, recv_sem, out_sem):
    me = lax.axis_index("slab")
    channels = cur.shape[1]
    group = plane.shape[0] // (2 * TAPS * TAPS)
    rows = CHUNK_X * extent_y
    chunks = extent_x // CHUNK_X
    halo = 2 * extent_y
    hid = expand.shape[1]

    loads = [
        pltpu.make_async_copy(src, dst, load_sem.at[k])
        for k, (src, dst) in enumerate(
            ((plane_hbm, plane), (vol_hbm, cur), (expand_hbm, expand), (down_hbm, down)))
    ]
    for load in loads:
        load.start()

    reach = [(layer, side, me + (d if side == 0 else -d))
             for layer, d in enumerate(DILATIONS) for side in (0, 1)]

    def inside(other):
        return jnp.logical_and(other >= 0, other < devices)

    barrier = pltpu.get_barrier_semaphore()
    for _, _, other in reach:
        @pl.when(inside(other))
        def _():
            pl.semaphore_signal(barrier, inc=1, device_id={"slab": other}, device_id_type=pl.DeviceIdType.MESH)

    row_group = lax.broadcasted_iota(jnp.int32, (channels, channels), 0) // group
    column_group = lax.broadcasted_iota(jnp.int32, (channels, channels), 1) // group
    mask[...] = jnp.where(row_group == column_group, 1.0, 0.0).astype(jnp.bfloat16)
    edge = jnp.zeros((halo, TAPS * channels), jnp.bfloat16)
    window[:halo, :] = edge
    window[halo + extent_x * extent_y:, :] = edge

    for layer, side, other in reach:
        source = me - (other - me)
        landing = lower if side == 0 else upper

        @pl.when(jnp.logical_not(inside(source)))
        def _():
            landing[layer] = jnp.zeros(landing.shape[1:], jnp.bfloat16)

    def build_taps(layer):
        def one(t, carry):
            tap = plane[pl.ds(pl.multiple_of((layer * TAPS * TAPS + t) * group, group), group), :]
            tiled = jnp.concatenate([tap] * (channels // group), axis=0)
            taps[pl.ds(pl.multiple_of(t * channels, channels), channels), :] = tiled * mask[...]
            return carry
        lax.fori_loop(0, TAPS * TAPS, one, 0)

    def fill(at, value):
        y = lax.broadcasted_iota(jnp.int32, (rows, channels), 0) % extent_y
        for dy in range(TAPS):
            shift = dy - 2
            if shift == 0:
                moved = value
            else:
                moved = pltpu.roll(value, (-shift) % rows, 0)
                inside_y = jnp.logical_and(y + shift >= 0, y + shift < extent_y)
                moved = jnp.where(inside_y, moved, 0.0)
            window[pl.ds(at + halo, rows), dy * channels:(dy + 1) * channels] = moved.astype(jnp.bfloat16)

    def mix(layer, at):
        total = None
        for dx in range(TAPS):
            part = jnp.dot(
                window[pl.ds(pl.multiple_of(at + dx * extent_y, extent_y), rows), :],
                taps[dx * TAPS * channels:(dx + 1) * TAPS * channels, :],
                preferred_element_type=jnp.float32)
            total = part if total is None else total + part
        scale = lax.rsqrt(jnp.mean(total * total, axis=-1, keepdims=True) + EPSILON)
        gain = gain_ref[...].astype(jnp.float32)[layer:layer + 1] * 0.5
        half = (total * scale * gain).astype(jnp.bfloat16)
        h = jnp.dot(half, expand[layer * channels:(layer + 1) * channels, :], preferred_element_type=jnp.float32)
        hidden = (h + h * jnp.tanh(h)).astype(jnp.bfloat16)
        out = jnp.dot(hidden, down[layer * hid:(layer + 1) * hid, :], preferred_element_type=jnp.float32)
        mixed[layer, pl.ds(at, rows), :] = out.astype(jnp.bfloat16)

    def copy(layer, side, chunk):
        at = pl.multiple_of(chunk * rows, rows)
        landing = lower if side == 0 else upper
        d = DILATIONS[layer]
        return pltpu.make_async_remote_copy(
            src_ref=mixed.at[layer, pl.ds(at, rows), :],
            dst_ref=landing.at[layer, pl.ds(at, rows), :],
            send_sem=send_sem.at[layer, side, chunk],
            recv_sem=recv_sem.at[layer, side, chunk],
            device_id={"slab": me + (d if side == 0 else -d)},
            device_id_type=pl.DeviceIdType.MESH)

    def send(layer, chunk):
        for side in (0, 1):
            d = DILATIONS[layer]

            @pl.when(inside(me + (d if side == 0 else -d)))
            def _():
                copy(layer, side, chunk).start()

    def receive(layer, chunk):
        for side in (0, 1):
            d = DILATIONS[layer]

            @pl.when(inside(me - (d if side == 0 else -d)))
            def _():
                copy(layer, side, chunk).wait_recv()

    def combine(layer, at):
        coeffs = depth_ref[layer].astype(jnp.float32)
        here = pl.ds(at, rows)
        term = (coeffs[0:1] * lower[layer, here, :].astype(jnp.float32)
                + coeffs[1:2] * mixed[layer, here, :].astype(jnp.float32)
                + coeffs[2:3] * upper[layer, here, :].astype(jnp.float32))
        term = term.astype(jnp.bfloat16).astype(jnp.float32)
        return (cur[here, :].astype(jnp.float32) + term).astype(jnp.bfloat16)

    loads[0].wait()
    build_taps(0)
    loads[1].wait()

    def first_fill(i, carry):
        at = pl.multiple_of(i * rows, rows)
        fill(at, cur[pl.ds(at, rows), :].astype(jnp.float32))
        return carry
    lax.fori_loop(0, chunks, first_fill, 0)
    loads[2].wait()
    loads[3].wait()
    pl.semaphore_wait(barrier, sum(inside(other).astype(jnp.int32) for _, _, other in reach))

    def first(i, carry):
        mix(0, pl.multiple_of(i * rows, rows))
        send(0, i)
        return carry
    lax.fori_loop(0, chunks, first, 0)

    build_taps(1)

    def second(i, carry):
        @pl.when(i < chunks)
        def _():
            receive(0, i)
            at = pl.multiple_of(i * rows, rows)
            value = combine(0, at)
            cur[pl.ds(at, rows), :] = value
            fill(at, value.astype(jnp.float32))

        @pl.when(i >= 1)
        def _():
            mix(1, pl.multiple_of((i - 1) * rows, rows))
            send(1, i - 1)
        return carry
    lax.fori_loop(0, chunks + 1, second, 0)

    def store(i):
        at = pl.multiple_of(i * rows, rows)
        return pltpu.make_async_copy(result.at[pl.ds(at, rows), :], out_hbm.at[pl.ds(at, rows), :], out_sem.at[i])

    def last(i, carry):
        receive(1, i)
        at = pl.multiple_of(i * rows, rows)
        result[pl.ds(at, rows), :] = combine(1, at)
        store(i).start()
        return carry
    lax.fori_loop(0, chunks, last, 0)

    def drain(i, carry):
        store(i).wait()
        for layer, side, other in reach:
            @pl.when(inside(other))
            def _():
                copy(layer, side, i).wait_send()
        return carry
    lax.fori_loop(0, chunks, drain, 0)


def shards(devices, volume, plane_weight, norm_gain, expand_weight, down_weight, depth_weight):
    slab_depth, extent_x, extent_y, channels = volume.shape
    layers, _, _, group, _ = plane_weight.shape
    hid = expand_weight.shape[2]
    cells = extent_x * extent_y
    chunks = extent_x // CHUNK_X
    bf16 = jnp.bfloat16
    whole = pl.BlockSpec(memory_space=pltpu.VMEM)
    far = pl.BlockSpec(memory_space=pl.ANY)
    out = pl.pallas_call(
        functools.partial(kernel, devices, extent_x, extent_y),
        out_shape=jax.ShapeDtypeStruct((cells, channels), bf16),
        in_specs=[far, far, whole, far, far, whole],
        out_specs=far,
        scratch_shapes=[
            pltpu.VMEM((cells, channels), bf16),
            pltpu.VMEM((layers * TAPS * TAPS * group, channels), bf16),
            pltpu.VMEM((layers * channels, hid), bf16),
            pltpu.VMEM((layers * hid, channels), bf16),
            pltpu.VMEM((channels, channels), bf16),
            pltpu.VMEM((TAPS * TAPS * channels, channels), bf16),
            pltpu.VMEM((cells + 4 * extent_y, TAPS * channels), bf16),
            pltpu.VMEM((layers, cells, channels), bf16),
            pltpu.VMEM((layers, cells, channels), bf16),
            pltpu.VMEM((layers, cells, channels), bf16),
            pltpu.VMEM((cells, channels), bf16),
            pltpu.SemaphoreType.DMA((4,)),
            pltpu.SemaphoreType.DMA((layers, 2, chunks)),
            pltpu.SemaphoreType.DMA((layers, 2, chunks)),
            pltpu.SemaphoreType.DMA((chunks,)),
        ],
        compiler_params=pltpu.CompilerParams(
            collective_id=0, has_side_effects=True, vmem_limit_bytes=48 * 1024 * 1024),
        cost_estimate=pl.CostEstimate(flops=9 * 10**9, bytes_accessed=5 * 10**6, transcendentals=2 * 10**6),
    )(
        volume.reshape(cells, channels),
        plane_weight.reshape(layers * TAPS * TAPS * group, channels),
        norm_gain,
        expand_weight.reshape(layers * channels, hid),
        down_weight.reshape(layers * hid, channels),
        depth_weight,
    )
    return out.reshape(volume.shape)


def solution(mesh):
    placed = (P(("parts", "slab"), None, None, None), P(), P(), P(), P(), P())
    return jax.shard_map(
        functools.partial(shards, mesh.shape["slab"]),
        mesh=mesh,
        in_specs=placed,
        out_specs=P(("parts", "slab"), None, None, None),
        check_vma=False,
    )
```

```python
import functools

import jax
import jax.numpy as jnp
from jax import lax
from jax.experimental import pallas as pl
from jax.experimental.pallas import tpu as pltpu
from jax.sharding import PartitionSpec as P

DILATIONS = (1, 4)
TAPS = 5
EPSILON = 1e-06
CHUNK_X = 4


def kernel(devices, extent_x, extent_y, vol_hbm, plane_hbm, gain_ref, expand_hbm, down_hbm, depth_ref, out_hbm,
           cur, plane, expand, down, mask, taps, window, mixed, lower, upper, result,
           load_sem, send_sem, recv_sem, out_sem):
    me = lax.axis_index("slab")
    channels = cur.shape[1]
    group = plane.shape[0] // (2 * TAPS * TAPS)
    rows = CHUNK_X * extent_y
    chunks = extent_x // CHUNK_X
    halo = 2 * extent_y
    hid = expand.shape[1]

    loads = [
        pltpu.make_async_copy(src, dst, load_sem.at[k])
        for k, (src, dst) in enumerate(
            ((plane_hbm, plane), (vol_hbm, cur), (expand_hbm, expand), (down_hbm, down)))
    ]
    for load in loads:
        load.start()

    reach = [(layer, side, me + (d if side == 0 else -d))
             for layer, d in enumerate(DILATIONS) for side in (0, 1)]

    def inside(other):
        return jnp.logical_and(other >= 0, other < devices)

    barrier = pltpu.get_barrier_semaphore()
    for _, _, other in reach:
        @pl.when(inside(other))
        def _():
            pl.semaphore_signal(barrier, inc=1, device_id={"slab": other}, device_id_type=pl.DeviceIdType.MESH)

    row_group = lax.broadcasted_iota(jnp.int32, (channels, channels), 0) // group
    column_group = lax.broadcasted_iota(jnp.int32, (channels, channels), 1) // group
    mask[...] = jnp.where(row_group == column_group, 1.0, 0.0).astype(jnp.bfloat16)
    edge = jnp.zeros((halo, TAPS * channels), jnp.bfloat16)
    window[:halo, :] = edge
    window[halo + extent_x * extent_y:, :] = edge

    for layer, side, other in reach:
        source = me - (other - me)
        landing = lower if side == 0 else upper

        @pl.when(jnp.logical_not(inside(source)))
        def _():
            landing[layer] = jnp.zeros(landing.shape[1:], jnp.bfloat16)

    def build_taps(layer):
        def one(t, carry):
            tap = plane[pl.ds(pl.multiple_of((layer * TAPS * TAPS + t) * group, group), group), :]
            tiled = jnp.concatenate([tap] * (channels // group), axis=0)
            taps[pl.ds(pl.multiple_of(t * channels, channels), channels), :] = tiled * mask[...]
            return carry
        lax.fori_loop(0, TAPS * TAPS, one, 0)

    def fill(at, value):
        y = lax.broadcasted_iota(jnp.int32, (rows, channels), 0) % extent_y
        for dy in range(TAPS):
            shift = dy - 2
            if shift == 0:
                moved = value
            else:
                moved = pltpu.roll(value, (-shift) % rows, 0)
                inside_y = jnp.logical_and(y + shift >= 0, y + shift < extent_y)
                moved = jnp.where(inside_y, moved, 0.0)
            window[pl.ds(at + halo, rows), dy * channels:(dy + 1) * channels] = moved.astype(jnp.bfloat16)

    def mix(layer, at):
        total = None
        for dx in range(TAPS):
            part = jnp.dot(
                window[pl.ds(pl.multiple_of(at + dx * extent_y, extent_y), rows), :],
                taps[dx * TAPS * channels:(dx + 1) * TAPS * channels, :],
                preferred_element_type=jnp.float32)
            total = part if total is None else total + part
        scale = lax.rsqrt(jnp.mean(total * total, axis=-1, keepdims=True) + EPSILON)
        gain = gain_ref[...].astype(jnp.float32)[layer:layer + 1] * 0.5
        half = (total * scale * gain).astype(jnp.bfloat16)
        h = jnp.dot(half, expand[layer * channels:(layer + 1) * channels, :], preferred_element_type=jnp.float32)
        hidden = (h + h * jnp.tanh(h)).astype(jnp.bfloat16)
        out = jnp.dot(hidden, down[layer * hid:(layer + 1) * hid, :], preferred_element_type=jnp.float32)
        mixed[layer, pl.ds(at, rows), :] = out.astype(jnp.bfloat16)

    def copy(layer, side, chunk):
        at = pl.multiple_of(chunk * rows, rows)
        landing = lower if side == 0 else upper
        d = DILATIONS[layer]
        return pltpu.make_async_remote_copy(
            src_ref=mixed.at[layer, pl.ds(at, rows), :],
            dst_ref=landing.at[layer, pl.ds(at, rows), :],
            send_sem=send_sem.at[layer, side, chunk],
            recv_sem=recv_sem.at[layer, side, chunk],
            device_id={"slab": me + (d if side == 0 else -d)},
            device_id_type=pl.DeviceIdType.MESH)

    def send(layer, chunk):
        for side in (0, 1):
            d = DILATIONS[layer]

            @pl.when(inside(me + (d if side == 0 else -d)))
            def _():
                copy(layer, side, chunk).start()

    def receive(layer, chunk):
        for side in (0, 1):
            d = DILATIONS[layer]

            @pl.when(inside(me - (d if side == 0 else -d)))
            def _():
                copy(layer, side, chunk).wait_recv()

    def combine(layer, at):
        coeffs = [depth_ref[k].astype(jnp.float32)[layer:layer + 1] for k in range(3)]
        here = pl.ds(at, rows)
        term = (coeffs[0] * lower[layer, here, :].astype(jnp.float32)
                + coeffs[1] * mixed[layer, here, :].astype(jnp.float32)
                + coeffs[2] * upper[layer, here, :].astype(jnp.float32))
        term = term.astype(jnp.bfloat16).astype(jnp.float32)
        return (cur[here, :].astype(jnp.float32) + term).astype(jnp.bfloat16)

    loads[0].wait()
    build_taps(0)
    loads[1].wait()

    def first_fill(i, carry):
        at = pl.multiple_of(i * rows, rows)
        fill(at, cur[pl.ds(at, rows), :].astype(jnp.float32))
        return carry
    lax.fori_loop(0, chunks, first_fill, 0)
    loads[2].wait()
    loads[3].wait()
    pl.semaphore_wait(barrier, sum(inside(other).astype(jnp.int32) for _, _, other in reach))

    def first(i, carry):
        mix(0, pl.multiple_of(i * rows, rows))
        send(0, i)
        return carry
    lax.fori_loop(0, chunks, first, 0)

    build_taps(1)

    def second(i, carry):
        @pl.when(i < chunks)
        def _():
            receive(0, i)
            at = pl.multiple_of(i * rows, rows)
            value = combine(0, at)
            cur[pl.ds(at, rows), :] = value
            fill(at, value.astype(jnp.float32))

        @pl.when(i >= 1)
        def _():
            mix(1, pl.multiple_of((i - 1) * rows, rows))
            send(1, i - 1)
        return carry
    lax.fori_loop(0, chunks + 1, second, 0)

    def store(i):
        at = pl.multiple_of(i * rows, rows)
        return pltpu.make_async_copy(result.at[pl.ds(at, rows), :], out_hbm.at[pl.ds(at, rows), :], out_sem.at[i])

    def last(i, carry):
        receive(1, i)
        at = pl.multiple_of(i * rows, rows)
        result[pl.ds(at, rows), :] = combine(1, at)
        store(i).start()
        return carry
    lax.fori_loop(0, chunks, last, 0)

    def drain(i, carry):
        store(i).wait()
        for layer, side, other in reach:
            @pl.when(inside(other))
            def _():
                copy(layer, side, i).wait_send()
        return carry
    lax.fori_loop(0, chunks, drain, 0)


def shards(devices, volume, plane_weight, norm_gain, expand_weight, down_weight, depth_weight):
    slab_depth, extent_x, extent_y, channels = volume.shape
    layers, _, _, group, _ = plane_weight.shape
    hid = expand_weight.shape[2]
    cells = extent_x * extent_y
    chunks = extent_x // CHUNK_X
    bf16 = jnp.bfloat16
    whole = pl.BlockSpec(memory_space=pltpu.VMEM)
    far = pl.BlockSpec(memory_space=pl.ANY)
    out = pl.pallas_call(
        functools.partial(kernel, devices, extent_x, extent_y),
        out_shape=jax.ShapeDtypeStruct((cells, channels), bf16),
        in_specs=[far, far, whole, far, far, whole],
        out_specs=far,
        scratch_shapes=[
            pltpu.VMEM((cells, channels), bf16),
            pltpu.VMEM((layers * TAPS * TAPS * group, channels), bf16),
            pltpu.VMEM((layers * channels, hid), bf16),
            pltpu.VMEM((layers * hid, channels), bf16),
            pltpu.VMEM((channels, channels), bf16),
            pltpu.VMEM((TAPS * TAPS * channels, channels), bf16),
            pltpu.VMEM((cells + 4 * extent_y, TAPS * channels), bf16),
            pltpu.VMEM((layers, cells, channels), bf16),
            pltpu.VMEM((layers, cells, channels), bf16),
            pltpu.VMEM((layers, cells, channels), bf16),
            pltpu.VMEM((cells, channels), bf16),
            pltpu.SemaphoreType.DMA((4,)),
            pltpu.SemaphoreType.DMA((layers, 2, chunks)),
            pltpu.SemaphoreType.DMA((layers, 2, chunks)),
            pltpu.SemaphoreType.DMA((chunks,)),
        ],
        compiler_params=pltpu.CompilerParams(
            collective_id=0, has_side_effects=True, vmem_limit_bytes=63 * 1024 * 1024),
        cost_estimate=pl.CostEstimate(flops=9 * 10**9, bytes_accessed=5 * 10**6, transcendentals=2 * 10**6),
    )(
        volume.reshape(cells, channels),
        plane_weight.reshape(layers * TAPS * TAPS * group, channels),
        norm_gain,
        expand_weight.reshape(layers * channels, hid),
        down_weight.reshape(layers * hid, channels),
        depth_weight.transpose(1, 0, 2),
    )
    return out.reshape(volume.shape)


def solution(mesh):
    placed = (P(("parts", "slab"), None, None, None), P(), P(), P(), P(), P())
    return jax.shard_map(
        functools.partial(shards, mesh.shape["slab"]),
        mesh=mesh,
        in_specs=placed,
        out_specs=P(("parts", "slab"), None, None, None),
        check_vma=False,
    )
```

```python
import functools

import jax
import jax.numpy as jnp
from jax import lax
from jax.experimental import pallas as pl
from jax.experimental.pallas import tpu as pltpu
from jax.sharding import PartitionSpec as P

DILATIONS = (1, 4)
TAPS = 5
EPSILON = 1e-06
CHUNK_X = 4
PACK = 4
CONV_CHUNKS = 2


def kernel(devices, extent_x, extent_y, vol_hbm, plane_hbm, gain_ref, expand_hbm, down_hbm, depth_ref, out_hbm,
           vol, stage, cur, plane, expand, down, taps, window, normed, mixed, lower, upper, result,
           load_sem, send_sem, recv_sem, out_sem):
    me = lax.axis_index("slab")
    channels = cur.shape[1]
    group = plane.shape[0] // (2 * TAPS * TAPS)
    blocks = extent_y // PACK
    plane_rows = CHUNK_X * blocks
    rows = PACK * plane_rows
    chunks = extent_x // CHUNK_X
    halo = 2 * blocks
    hid = expand.shape[1]
    half = channels // 2
    quarter = channels // PACK
    depth = 2 * channels
    bf16, f32 = jnp.bfloat16, jnp.float32

    loads = [
        pltpu.make_async_copy(src, dst, load_sem.at[k])
        for k, (src, dst) in enumerate(
            ((plane_hbm, plane), (vol_hbm, vol), (expand_hbm, expand), (down_hbm, down)))
    ]
    for load in loads:
        load.start()

    reach = [(layer, side, me + (d if side == 0 else -d))
             for layer, d in enumerate(DILATIONS) for side in (0, 1)]

    def inside(other):
        return jnp.logical_and(other >= 0, other < devices)

    barrier = pltpu.get_barrier_semaphore()
    for _, _, other in reach:
        @pl.when(inside(other))
        def _():
            pl.semaphore_signal(barrier, inc=1, device_id={"slab": other}, device_id_type=pl.DeviceIdType.MESH)

    edge = jnp.zeros((halo, PACK * depth), bf16)
    window[:halo, :] = edge
    window[halo + extent_x * blocks:, :] = edge

    for layer, side, other in reach:
        source = me - (other - me)
        landing = lower if side == 0 else upper

        @pl.when(jnp.logical_not(inside(source)))
        def _():
            landing[layer] = jnp.zeros(landing.shape[1:], bf16)

    def is_low(count):
        return lax.broadcasted_iota(jnp.int32, (count, half), 1) < quarter

    def swap(value):
        return pltpu.roll(value, quarter, 1)

    lane_group = lax.broadcasted_iota(jnp.int32, (group, half), 1) % quarter // group
    group_mask = [jnp.where(lane_group == g, 1.0, 0.0).astype(bf16) for g in range(quarter // group)]

    def clear(t, carry):
        for v, start in ((0, 6 * quarter), (1, 0)):
            taps[pl.ds(pl.multiple_of(t * depth + start, 2 * quarter), 2 * quarter), v * half:(v + 1) * half] = (
                jnp.zeros((2 * quarter, half), bf16))
        return carry
    lax.fori_loop(0, TAPS * PACK, clear, 0)

    def build_taps(layer):
        def one(dx, carry):
            base = (layer * TAPS + dx) * TAPS * group
            for h in range(2):
                straight = [
                    plane[pl.ds(pl.multiple_of(base + dy * group, group), group), h * half:(h + 1) * half].astype(f32)
                    for dy in range(TAPS)]
                swapped = [swap(value) for value in straight]
                zero = jnp.zeros((group, half), f32)
                for odd in range(2):
                    left, right = (swapped, straight) if odd else (straight, swapped)
                    at = pl.multiple_of((dx * PACK + 2 * h + odd) * depth, depth)
                    for k in range(TAPS + 1):
                        pair = jnp.where(
                            is_low(group), left[k] if k < TAPS else zero, right[k - 1] if k > 0 else zero).astype(bf16)
                        for g, only in enumerate(group_mask):
                            tile = pair * only
                            for v in range(2):
                                taps[pl.ds(at + (k + 2 * v) * quarter + g * group, group),
                                     v * half:(v + 1) * half] = tile
            return carry
        lax.fori_loop(0, TAPS, one, 0)

    def fill(chunk, planes):
        block = lax.broadcasted_iota(jnp.int32, (plane_rows, channels), 0) % blocks

        def before(value):
            return jnp.where(block == 0, 0.0, pltpu.roll(value, 1, 0))

        def after(value):
            return jnp.where(block == blocks - 1, 0.0, pltpu.roll(value, plane_rows - 1, 0))

        y = [before(planes[2]), before(planes[3]), *planes, after(planes[0]), after(planes[1])]
        here = pl.ds(pl.multiple_of(chunk * plane_rows + halo, halo), plane_rows)
        low = is_low(plane_rows)
        for k in range(0, 2 * PACK, 2):
            for h in range(2):
                a = y[k][:, h * half:(h + 1) * half]
                b = y[k + 1][:, h * half:(h + 1) * half]
                at = 2 * h * depth + k * quarter
                window[here, at:at + half] = jnp.where(low, a, swap(b)).astype(bf16)
                window[here, at + depth:at + depth + half] = jnp.where(low, swap(a), b).astype(bf16)

    ones = jnp.where(
        lax.broadcasted_iota(jnp.int32, (channels, channels), 0) // quarter
        == lax.broadcasted_iota(jnp.int32, (channels, channels), 1) // quarter, 1.0, 0.0).astype(bf16)

    def conv(layer, first_chunk, count):
        size = count * plane_rows
        at = first_chunk * plane_rows
        totals = []
        for q in range(PACK):
            total = None
            for dx in range(TAPS):
                part = jnp.dot(
                    window[at + dx * blocks:at + dx * blocks + size, q * depth:(q + 1) * depth],
                    taps[(dx * PACK + q) * depth:(dx * PACK + q + 1) * depth, :],
                    preferred_element_type=f32)
                total = part if total is None else total + part
            totals.append(total)
        squares = sum(total * total for total in totals)
        coarse = squares.astype(bf16)
        fine = (squares - coarse.astype(f32)).astype(bf16)
        mean = (jnp.dot(coarse, ones, preferred_element_type=f32)
                + jnp.dot(fine, ones, preferred_element_type=f32)) * (1.0 / channels)
        scale = lax.rsqrt(mean + EPSILON)
        gain = gain_ref[...].astype(f32)[layer:layer + 1] * 0.5
        low = is_low(size)
        for h in range(2):
            pair = gain[:, h * half:(h + 1) * half]
            other = swap(jnp.broadcast_to(pair, (8, half)))[0:1]
            low_row = is_low(1)
            even = jnp.where(low_row, pair, other)
            odd = jnp.where(low_row, other, pair)
            for v in range(2):
                lanes = slice(v * half, (v + 1) * half)
                a = totals[2 * h][:, lanes] * scale[:, lanes] * even
                b = totals[2 * h + 1][:, lanes] * scale[:, lanes] * odd
                for j, value in ((2 * v, jnp.where(low, a, swap(b))), (2 * v + 1, jnp.where(low, swap(a), b))):
                    value = value.astype(bf16)
                    for c in range(count):
                        to = (first_chunk + c) * rows + j * plane_rows
                        normed[to:to + plane_rows, h * half:(h + 1) * half] = (
                            value[c * plane_rows:(c + 1) * plane_rows])

    def mix(layer, chunk):
        here = pl.ds(pl.multiple_of(chunk * rows, rows), rows)
        h = jnp.dot(normed[here, :], expand[layer * channels:(layer + 1) * channels, :],
                    preferred_element_type=f32).astype(bf16)
        hidden = h + h * jnp.tanh(h)
        out = jnp.dot(hidden, down[layer * hid:(layer + 1) * hid, :], preferred_element_type=f32)
        mixed[layer, here, :] = out.astype(bf16)

    def copy(layer, side, chunk):
        at = pl.multiple_of(chunk * rows, rows)
        landing = lower if side == 0 else upper
        d = DILATIONS[layer]
        return pltpu.make_async_remote_copy(
            src_ref=mixed.at[layer, pl.ds(at, rows), :],
            dst_ref=landing.at[layer, pl.ds(at, rows), :],
            send_sem=send_sem.at[layer, side, chunk],
            recv_sem=recv_sem.at[layer, side, chunk],
            device_id={"slab": me + (d if side == 0 else -d)},
            device_id_type=pl.DeviceIdType.MESH)

    def send(layer, chunk):
        for side in (0, 1):
            d = DILATIONS[layer]

            @pl.when(inside(me + (d if side == 0 else -d)))
            def _():
                copy(layer, side, chunk).start()

    def receive(layer, chunk):
        for side in (0, 1):
            d = DILATIONS[layer]

            @pl.when(inside(me - (d if side == 0 else -d)))
            def _():
                copy(layer, side, chunk).wait_recv()

    def combine(layer, at):
        coeffs = [depth_ref[k].astype(f32)[layer:layer + 1] for k in range(3)]
        here = pl.ds(at, rows)
        term = (coeffs[0] * lower[layer, here, :].astype(f32)
                + coeffs[1] * mixed[layer, here, :].astype(f32)
                + coeffs[2] * upper[layer, here, :].astype(f32))
        term = term.astype(bf16).astype(f32)
        return (cur[here, :].astype(f32) + term).astype(bf16).astype(f32)

    def mix_and_send(layer, first_chunk, count):
        def one(i, carry):
            mix(layer, i)
            send(layer, i)
            return carry
        lax.fori_loop(first_chunk, first_chunk + count, one, 0)

    loads[1].wait()

    def first_fill(i, carry):
        at = pl.multiple_of(i * rows, rows)
        value = vol[pl.ds(at, rows), :].astype(f32)
        for h in range(2):
            stage[h, pl.ds(at, rows), :] = value[:, h * half:(h + 1) * half]
        planes = [
            jnp.concatenate([stage[h, pl.ds(at + j, plane_rows, stride=PACK), :] for h in range(2)], axis=1)
            for j in range(PACK)]
        for j in range(PACK):
            cur[pl.ds(at + j * plane_rows, plane_rows), :] = planes[j].astype(bf16)
        fill(i, planes)
        return carry
    lax.fori_loop(0, chunks, first_fill, 0)
    loads[0].wait()
    build_taps(0)
    conv(0, 0, chunks)
    loads[2].wait()
    loads[3].wait()
    pl.semaphore_wait(barrier, sum(inside(other).astype(jnp.int32) for _, _, other in reach))
    mix_and_send(0, 0, chunks)

    build_taps(1)

    def refill(i, carry):
        receive(0, i)
        at = pl.multiple_of(i * rows, rows)
        value = combine(0, at)
        cur[pl.ds(at, rows), :] = value.astype(bf16)
        fill(i, [value[j * plane_rows:(j + 1) * plane_rows] for j in range(PACK)])
        return carry

    filled = 0
    for start in range(0, chunks, CONV_CHUNKS):
        need = min(start + CONV_CHUNKS + 1, chunks)
        lax.fori_loop(filled, need, refill, 0)
        filled = need
        conv(1, start, CONV_CHUNKS)
        mix_and_send(1, start, CONV_CHUNKS)

    def store(i):
        at = pl.multiple_of(i * rows, rows)
        return pltpu.make_async_copy(result.at[pl.ds(at, rows), :], out_hbm.at[pl.ds(at, rows), :], out_sem.at[i])

    def last(i, carry):
        receive(1, i)
        at = pl.multiple_of(i * rows, rows)
        value = combine(1, at)
        for h in range(2):
            for j in range(PACK):
                stage[h, pl.ds(at + j, plane_rows, stride=PACK), :] = (
                    value[j * plane_rows:(j + 1) * plane_rows, h * half:(h + 1) * half])
            result[pl.ds(at, rows), h * half:(h + 1) * half] = stage[h, pl.ds(at, rows), :].astype(bf16)
        store(i).start()
        return carry
    lax.fori_loop(0, chunks, last, 0)

    def drain(i, carry):
        store(i).wait()
        for layer, side, other in reach:
            @pl.when(inside(other))
            def _():
                copy(layer, side, i).wait_send()
        return carry
    lax.fori_loop(0, chunks, drain, 0)


def shards(devices, volume, plane_weight, norm_gain, expand_weight, down_weight, depth_weight):
    slab_depth, extent_x, extent_y, channels = volume.shape
    layers, _, _, group, _ = plane_weight.shape
    hid = expand_weight.shape[2]
    cells = extent_x * extent_y
    chunks = extent_x // CHUNK_X
    bf16 = jnp.bfloat16
    whole = pl.BlockSpec(memory_space=pltpu.VMEM)
    far = pl.BlockSpec(memory_space=pl.ANY)
    out = pl.pallas_call(
        functools.partial(kernel, devices, extent_x, extent_y),
        out_shape=jax.ShapeDtypeStruct((cells, channels), bf16),
        in_specs=[far, far, whole, far, far, whole],
        out_specs=far,
        scratch_shapes=[
            pltpu.VMEM((cells, channels), bf16),
            pltpu.VMEM((2, cells, channels // 2), jnp.float32),
            pltpu.VMEM((cells, channels), bf16),
            pltpu.VMEM((layers * TAPS * TAPS * group, channels), bf16),
            pltpu.VMEM((layers * channels, hid), bf16),
            pltpu.VMEM((layers * hid, channels), bf16),
            pltpu.VMEM((TAPS * PACK * 2 * channels, channels), bf16),
            pltpu.VMEM(((extent_x + 4) * extent_y // PACK, PACK * 2 * channels), bf16),
            pltpu.VMEM((cells, channels), bf16),
            pltpu.VMEM((layers, cells, channels), bf16),
            pltpu.VMEM((layers, cells, channels), bf16),
            pltpu.VMEM((layers, cells, channels), bf16),
            pltpu.VMEM((cells, channels), bf16),
            pltpu.SemaphoreType.DMA((4,)),
            pltpu.SemaphoreType.DMA((layers, 2, chunks)),
            pltpu.SemaphoreType.DMA((layers, 2, chunks)),
            pltpu.SemaphoreType.DMA((chunks,)),
        ],
        compiler_params=pltpu.CompilerParams(
            collective_id=0, has_side_effects=True, vmem_limit_bytes=63 * 1024 * 1024),
        cost_estimate=pl.CostEstimate(flops=9 * 10**9, bytes_accessed=5 * 10**6, transcendentals=2 * 10**6),
    )(
        volume.reshape(cells, channels),
        plane_weight.reshape(layers * TAPS * TAPS * group, channels),
        norm_gain,
        expand_weight.reshape(layers * channels, hid),
        down_weight.reshape(layers * hid, channels),
        depth_weight.transpose(1, 0, 2),
    )
    return out.reshape(volume.shape)


def solution(mesh):
    placed = (P(("parts", "slab"), None, None, None), P(), P(), P(), P(), P())
    return jax.shard_map(
        functools.partial(shards, mesh.shape["slab"]),
        mesh=mesh,
        in_specs=placed,
        out_specs=P(("parts", "slab"), None, None, None),
        check_vma=False,
    )
```

```python
import functools

import jax
import jax.numpy as jnp
from jax import lax
from jax.experimental import pallas as pl
from jax.experimental.pallas import tpu as pltpu
from jax.sharding import PartitionSpec as P

DILATIONS = (1, 4)
TAPS = 5
EPSILON = 1e-06
CHUNK_X = 2
PACK = 4
CONV_CHUNKS = 2


def kernel(devices, extent_x, extent_y, vol_hbm, plane_hbm, gain_ref, expand_hbm, down_hbm, depth_ref, out_hbm,
           vol, stage, cur, plane, expand, down, taps, window, normed, mixed, lower, upper, result,
           load_sem, send_sem, recv_sem, out_sem):
    me = lax.axis_index("slab")
    channels = cur.shape[1]
    group = plane.shape[0] // (2 * TAPS * TAPS)
    blocks = extent_y // PACK
    plane_rows = CHUNK_X * blocks
    rows = PACK * plane_rows
    chunks = extent_x // CHUNK_X
    halo = 2 * blocks
    hid = expand.shape[1]
    half = channels // 2
    quarter = channels // PACK
    depth = 2 * channels
    bf16, f32 = jnp.bfloat16, jnp.float32

    loads = [
        pltpu.make_async_copy(src, dst, load_sem.at[k])
        for k, (src, dst) in enumerate(
            ((plane_hbm, plane), (vol_hbm, vol), (expand_hbm, expand), (down_hbm, down)))
    ]
    for load in loads:
        load.start()

    reach = [(layer, side, me + (d if side == 0 else -d))
             for layer, d in enumerate(DILATIONS) for side in (0, 1)]

    def inside(other):
        return jnp.logical_and(other >= 0, other < devices)

    barrier = pltpu.get_barrier_semaphore()
    for _, _, other in reach:
        @pl.when(inside(other))
        def _():
            pl.semaphore_signal(barrier, inc=1, device_id={"slab": other}, device_id_type=pl.DeviceIdType.MESH)

    edge = jnp.zeros((halo, PACK * depth), bf16)
    window[:halo, :] = edge
    window[halo + extent_x * blocks:, :] = edge

    for layer, side, other in reach:
        source = me - (other - me)
        landing = lower if side == 0 else upper

        @pl.when(jnp.logical_not(inside(source)))
        def _():
            landing[layer] = jnp.zeros(landing.shape[1:], bf16)

    def is_low(count):
        return lax.broadcasted_iota(jnp.int32, (count, half), 1) < quarter

    def swap(value):
        return pltpu.roll(value, quarter, 1)

    lane_group = lax.broadcasted_iota(jnp.int32, (group, half), 1) % quarter // group
    group_mask = [jnp.where(lane_group == g, 1.0, 0.0).astype(bf16) for g in range(quarter // group)]

    def clear(t, carry):
        for v, start in ((0, 6 * quarter), (1, 0)):
            taps[pl.ds(pl.multiple_of(t * depth + start, 2 * quarter), 2 * quarter), v * half:(v + 1) * half] = (
                jnp.zeros((2 * quarter, half), bf16))
        return carry
    lax.fori_loop(0, TAPS * PACK, clear, 0)

    def build_taps(layer):
        def one(dx, carry):
            base = (layer * TAPS + dx) * TAPS * group
            for h in range(2):
                straight = [
                    plane[pl.ds(pl.multiple_of(base + dy * group, group), group), h * half:(h + 1) * half].astype(f32)
                    for dy in range(TAPS)]
                swapped = [swap(value) for value in straight]
                zero = jnp.zeros((group, half), f32)
                for odd in range(2):
                    left, right = (swapped, straight) if odd else (straight, swapped)
                    at = pl.multiple_of((dx * PACK + 2 * h + odd) * depth, depth)
                    for k in range(TAPS + 1):
                        pair = jnp.where(
                            is_low(group), left[k] if k < TAPS else zero, right[k - 1] if k > 0 else zero).astype(bf16)
                        for g, only in enumerate(group_mask):
                            tile = pair * only
                            for v in range(2):
                                taps[pl.ds(at + (k + 2 * v) * quarter + g * group, group),
                                     v * half:(v + 1) * half] = tile
            return carry
        lax.fori_loop(0, TAPS, one, 0)

    def fill(chunk, planes):
        block = lax.broadcasted_iota(jnp.int32, (plane_rows, channels), 0) % blocks

        def before(value):
            return jnp.where(block == 0, 0.0, pltpu.roll(value, 1, 0))

        def after(value):
            return jnp.where(block == blocks - 1, 0.0, pltpu.roll(value, plane_rows - 1, 0))

        y = [before(planes[2]), before(planes[3]), *planes, after(planes[0]), after(planes[1])]
        here = pl.ds(pl.multiple_of(chunk * plane_rows + halo, halo), plane_rows)
        low = is_low(plane_rows)
        for k in range(0, 2 * PACK, 2):
            for h in range(2):
                a = y[k][:, h * half:(h + 1) * half]
                b = y[k + 1][:, h * half:(h + 1) * half]
                at = 2 * h * depth + k * quarter
                window[here, at:at + half] = jnp.where(low, a, swap(b)).astype(bf16)
                window[here, at + depth:at + depth + half] = jnp.where(low, swap(a), b).astype(bf16)

    ones = jnp.where(
        lax.broadcasted_iota(jnp.int32, (channels, channels), 0) // quarter
        == lax.broadcasted_iota(jnp.int32, (channels, channels), 1) // quarter, 1.0, 0.0).astype(bf16)

    def conv(layer, first_chunk, count):
        size = count * plane_rows
        at = first_chunk * plane_rows
        totals = []
        for q in range(PACK):
            total = None
            for dx in range(TAPS):
                part = jnp.dot(
                    window[pl.ds(pl.multiple_of(at + dx * blocks, blocks), size), q * depth:(q + 1) * depth],
                    taps[(dx * PACK + q) * depth:(dx * PACK + q + 1) * depth, :],
                    preferred_element_type=f32)
                total = part if total is None else total + part
            totals.append(total)
        squares = sum(total * total for total in totals)
        coarse = squares.astype(bf16)
        fine = (squares - coarse.astype(f32)).astype(bf16)
        mean = (jnp.dot(coarse, ones, preferred_element_type=f32)
                + jnp.dot(fine, ones, preferred_element_type=f32)) * (1.0 / channels)
        scale = lax.rsqrt(mean + EPSILON)
        gain = gain_ref[...].astype(f32)[layer:layer + 1] * 0.5
        low = is_low(size)
        for h in range(2):
            pair = gain[:, h * half:(h + 1) * half]
            other = swap(jnp.broadcast_to(pair, (8, half)))[0:1]
            low_row = is_low(1)
            even = jnp.where(low_row, pair, other)
            odd = jnp.where(low_row, other, pair)
            for v in range(2):
                lanes = slice(v * half, (v + 1) * half)
                a = totals[2 * h][:, lanes] * scale[:, lanes] * even
                b = totals[2 * h + 1][:, lanes] * scale[:, lanes] * odd
                for j, value in ((2 * v, jnp.where(low, a, swap(b))), (2 * v + 1, jnp.where(low, swap(a), b))):
                    value = value.astype(bf16)
                    for c in range(count):
                        to = pl.multiple_of((first_chunk + c) * rows + j * plane_rows, plane_rows)
                        normed[pl.ds(to, plane_rows), h * half:(h + 1) * half] = (
                            value[c * plane_rows:(c + 1) * plane_rows])

    def mix(layer, chunk):
        here = pl.ds(pl.multiple_of(chunk * rows, rows), rows)
        h = jnp.dot(normed[here, :], expand[layer * channels:(layer + 1) * channels, :],
                    preferred_element_type=f32).astype(bf16)
        hidden = h + h * jnp.tanh(h)
        out = jnp.dot(hidden, down[layer * hid:(layer + 1) * hid, :], preferred_element_type=f32)
        mixed[layer, here, :] = out.astype(bf16)

    def copy(layer, side, chunk):
        at = pl.multiple_of(chunk * rows, rows)
        landing = lower if side == 0 else upper
        d = DILATIONS[layer]
        return pltpu.make_async_remote_copy(
            src_ref=mixed.at[layer, pl.ds(at, rows), :],
            dst_ref=landing.at[layer, pl.ds(at, rows), :],
            send_sem=send_sem.at[layer, side, chunk],
            recv_sem=recv_sem.at[layer, side, chunk],
            device_id={"slab": me + (d if side == 0 else -d)},
            device_id_type=pl.DeviceIdType.MESH)

    def send(layer, chunk):
        for side in (0, 1):
            d = DILATIONS[layer]

            @pl.when(inside(me + (d if side == 0 else -d)))
            def _():
                copy(layer, side, chunk).start()

    def receive(layer, chunk):
        for side in (0, 1):
            d = DILATIONS[layer]

            @pl.when(inside(me - (d if side == 0 else -d)))
            def _():
                copy(layer, side, chunk).wait_recv()

    def combine(layer, at):
        coeffs = [depth_ref[k].astype(f32)[layer:layer + 1] for k in range(3)]
        here = pl.ds(at, rows)
        term = (coeffs[0] * lower[layer, here, :].astype(f32)
                + coeffs[1] * mixed[layer, here, :].astype(f32)
                + coeffs[2] * upper[layer, here, :].astype(f32))
        term = term.astype(bf16).astype(f32)
        return (cur[here, :].astype(f32) + term).astype(bf16).astype(f32)

    def mix_and_send(layer, first_chunk, count):
        def one(i, carry):
            mix(layer, i)
            send(layer, i)
            return carry
        lax.fori_loop(first_chunk, first_chunk + count, one, 0)

    loads[1].wait()

    def first_fill(i, carry):
        at = pl.multiple_of(i * rows, rows)
        value = vol[pl.ds(at, rows), :].astype(f32)
        for h in range(2):
            stage[h, pl.ds(at, rows), :] = value[:, h * half:(h + 1) * half]
        planes = [
            jnp.concatenate([stage[h, pl.ds(at + j, plane_rows, stride=PACK), :] for h in range(2)], axis=1)
            for j in range(PACK)]
        for j in range(PACK):
            cur[pl.ds(at + j * plane_rows, plane_rows), :] = planes[j].astype(bf16)
        fill(i, planes)
        return carry
    lax.fori_loop(0, chunks, first_fill, 0)
    loads[0].wait()
    build_taps(0)
    conv(0, 0, chunks)
    loads[2].wait()
    loads[3].wait()
    pl.semaphore_wait(barrier, sum(inside(other).astype(jnp.int32) for _, _, other in reach))
    mix_and_send(0, 0, chunks)

    build_taps(1)

    def refill(i, carry):
        receive(0, i)
        at = pl.multiple_of(i * rows, rows)
        value = combine(0, at)
        cur[pl.ds(at, rows), :] = value.astype(bf16)
        fill(i, [value[j * plane_rows:(j + 1) * plane_rows] for j in range(PACK)])
        return carry

    lax.fori_loop(0, 1, refill, 0)

    def step(k, carry):
        start = k * CONV_CHUNKS
        lax.fori_loop(start + 1, jnp.minimum(start + 1 + CONV_CHUNKS, chunks), refill, 0)
        conv(1, start, CONV_CHUNKS)
        mix_and_send(1, start, CONV_CHUNKS)
        return carry
    lax.fori_loop(0, chunks // CONV_CHUNKS, step, 0)

    def store(i):
        at = pl.multiple_of(i * rows, rows)
        return pltpu.make_async_copy(result.at[pl.ds(at, rows), :], out_hbm.at[pl.ds(at, rows), :], out_sem.at[i])

    def last(i, carry):
        receive(1, i)
        at = pl.multiple_of(i * rows, rows)
        value = combine(1, at)
        for h in range(2):
            for j in range(PACK):
                stage[h, pl.ds(at + j, plane_rows, stride=PACK), :] = (
                    value[j * plane_rows:(j + 1) * plane_rows, h * half:(h + 1) * half])
            result[pl.ds(at, rows), h * half:(h + 1) * half] = stage[h, pl.ds(at, rows), :].astype(bf16)
        store(i).start()
        return carry
    lax.fori_loop(0, chunks, last, 0)

    def drain(i, carry):
        store(i).wait()
        for layer, side, other in reach:
            @pl.when(inside(other))
            def _():
                copy(layer, side, i).wait_send()
        return carry
    lax.fori_loop(0, chunks, drain, 0)


def shards(devices, volume, plane_weight, norm_gain, expand_weight, down_weight, depth_weight):
    slab_depth, extent_x, extent_y, channels = volume.shape
    layers, _, _, group, _ = plane_weight.shape
    hid = expand_weight.shape[2]
    cells = extent_x * extent_y
    chunks = extent_x // CHUNK_X
    bf16 = jnp.bfloat16
    whole = pl.BlockSpec(memory_space=pltpu.VMEM)
    far = pl.BlockSpec(memory_space=pl.ANY)
    out = pl.pallas_call(
        functools.partial(kernel, devices, extent_x, extent_y),
        out_shape=jax.ShapeDtypeStruct((cells, channels), bf16),
        in_specs=[far, far, whole, far, far, whole],
        out_specs=far,
        scratch_shapes=[
            pltpu.VMEM((cells, channels), bf16),
            pltpu.VMEM((2, cells, channels // 2), jnp.float32),
            pltpu.VMEM((cells, channels), bf16),
            pltpu.VMEM((layers * TAPS * TAPS * group, channels), bf16),
            pltpu.VMEM((layers * channels, hid), bf16),
            pltpu.VMEM((layers * hid, channels), bf16),
            pltpu.VMEM((TAPS * PACK * 2 * channels, channels), bf16),
            pltpu.VMEM(((extent_x + 4) * extent_y // PACK, PACK * 2 * channels), bf16),
            pltpu.VMEM((cells, channels), bf16),
            pltpu.VMEM((layers, cells, channels), bf16),
            pltpu.VMEM((layers, cells, channels), bf16),
            pltpu.VMEM((layers, cells, channels), bf16),
            pltpu.VMEM((cells, channels), bf16),
            pltpu.SemaphoreType.DMA((4,)),
            pltpu.SemaphoreType.DMA((layers, 2, chunks)),
            pltpu.SemaphoreType.DMA((layers, 2, chunks)),
            pltpu.SemaphoreType.DMA((chunks,)),
        ],
        compiler_params=pltpu.CompilerParams(
            collective_id=0, has_side_effects=True, vmem_limit_bytes=63 * 1024 * 1024),
        cost_estimate=pl.CostEstimate(flops=9 * 10**9, bytes_accessed=5 * 10**6, transcendentals=2 * 10**6),
    )(
        volume.reshape(cells, channels),
        plane_weight.reshape(layers * TAPS * TAPS * group, channels),
        norm_gain,
        expand_weight.reshape(layers * channels, hid),
        down_weight.reshape(layers * hid, channels),
        depth_weight.transpose(1, 0, 2),
    )
    return out.reshape(volume.shape)


def solution(mesh):
    placed = (P(("parts", "slab"), None, None, None), P(), P(), P(), P(), P())
    return jax.shard_map(
        functools.partial(shards, mesh.shape["slab"]),
        mesh=mesh,
        in_specs=placed,
        out_specs=P(("parts", "slab"), None, None, None),
        check_vma=False,
    )
```

```python
import functools

import jax
import jax.numpy as jnp
from jax import lax
from jax.experimental import pallas as pl
from jax.experimental.pallas import tpu as pltpu
from jax.sharding import PartitionSpec as P

DILATIONS = (1, 4)
TAPS = 5
EPSILON = 1e-06
CHUNK_X = 2
PACK = 4
CONV_CHUNKS = 2


def kernel(devices, extent_x, extent_y, vol_hbm, plane_hbm, gain_ref, expand_hbm, down_hbm, depth_ref, out_hbm,
           vol, stage, cur, plane, expand, down, taps, window, normed, mixed, lower, upper, result,
           load_sem, send_sem, recv_sem, out_sem):
    me = lax.axis_index("slab")
    channels = cur.shape[1]
    group = plane.shape[0] // (2 * TAPS * TAPS)
    blocks = extent_y // PACK
    plane_rows = CHUNK_X * blocks
    rows = PACK * plane_rows
    chunks = extent_x // CHUNK_X
    halo = 2 * blocks
    hid = expand.shape[1]
    half = channels // 2
    quarter = channels // PACK
    depth = 2 * channels
    bf16, f32 = jnp.bfloat16, jnp.float32

    loads = [
        pltpu.make_async_copy(src, dst, load_sem.at[k])
        for k, (src, dst) in enumerate(
            ((plane_hbm, plane), (vol_hbm, vol), (expand_hbm, expand), (down_hbm, down)))
    ]
    for load in loads:
        load.start()

    reach = [(layer, side, me + (d if side == 0 else -d))
             for layer, d in enumerate(DILATIONS) for side in (0, 1)]

    def inside(other):
        return jnp.logical_and(other >= 0, other < devices)

    barrier = pltpu.get_barrier_semaphore()
    for _, _, other in reach:
        @pl.when(inside(other))
        def _():
            pl.semaphore_signal(barrier, inc=1, device_id={"slab": other}, device_id_type=pl.DeviceIdType.MESH)

    edge = jnp.zeros((halo, PACK * depth), bf16)
    window[:halo, :] = edge
    window[halo + extent_x * blocks:, :] = edge

    for layer, side, other in reach:
        source = me - (other - me)
        landing = lower if side == 0 else upper

        @pl.when(jnp.logical_not(inside(source)))
        def _():
            landing[layer] = jnp.zeros(landing.shape[1:], bf16)

    def is_low(count):
        return lax.broadcasted_iota(jnp.int32, (count, half), 1) < quarter

    def swap(value):
        return pltpu.roll(value, quarter, 1)

    lane_group = lax.broadcasted_iota(jnp.int32, (group, half), 1) % quarter // group
    group_mask = [jnp.where(lane_group == g, 1.0, 0.0).astype(bf16) for g in range(quarter // group)]

    def clear(t, carry):
        for v, start in ((0, 6 * quarter), (1, 0)):
            taps[pl.ds(pl.multiple_of(t * depth + start, 2 * quarter), 2 * quarter), v * half:(v + 1) * half] = (
                jnp.zeros((2 * quarter, half), bf16))
        return carry
    lax.fori_loop(0, TAPS * PACK, clear, 0)

    def build_taps(layer):
        def one(dx, carry):
            base = (layer * TAPS + dx) * TAPS * group
            for h in range(2):
                straight = [
                    plane[pl.ds(pl.multiple_of(base + dy * group, group), group), h * half:(h + 1) * half].astype(f32)
                    for dy in range(TAPS)]
                swapped = [swap(value) for value in straight]
                zero = jnp.zeros((group, half), f32)
                for odd in range(2):
                    left, right = (swapped, straight) if odd else (straight, swapped)
                    at = pl.multiple_of((dx * PACK + 2 * h + odd) * depth, depth)
                    for k in range(TAPS + 1):
                        pair = jnp.where(
                            is_low(group), left[k] if k < TAPS else zero, right[k - 1] if k > 0 else zero).astype(bf16)
                        for g, only in enumerate(group_mask):
                            tile = pair * only
                            for v in range(2):
                                taps[pl.ds(at + (k + 2 * v) * quarter + g * group, group),
                                     v * half:(v + 1) * half] = tile
            return carry
        lax.fori_loop(0, TAPS, one, 0)

    def fill(chunk, planes):
        block = lax.broadcasted_iota(jnp.int32, (plane_rows, channels), 0) % blocks

        def before(value):
            return jnp.where(block == 0, 0.0, pltpu.roll(value, 1, 0))

        def after(value):
            return jnp.where(block == blocks - 1, 0.0, pltpu.roll(value, plane_rows - 1, 0))

        y = [before(planes[2]), before(planes[3]), *planes, after(planes[0]), after(planes[1])]
        here = pl.ds(pl.multiple_of(chunk * plane_rows + halo, halo), plane_rows)
        low = is_low(plane_rows)
        for k in range(0, 2 * PACK, 2):
            for h in range(2):
                a = y[k][:, h * half:(h + 1) * half]
                b = y[k + 1][:, h * half:(h + 1) * half]
                at = 2 * h * depth + k * quarter
                window[here, at:at + half] = jnp.where(low, a, swap(b)).astype(bf16)
                window[here, at + depth:at + depth + half] = jnp.where(low, swap(a), b).astype(bf16)

    ones = jnp.where(
        lax.broadcasted_iota(jnp.int32, (channels, channels), 0) // quarter
        == lax.broadcasted_iota(jnp.int32, (channels, channels), 1) // quarter, 1.0, 0.0).astype(bf16)

    def conv(layer, first_chunk, count):
        size = count * plane_rows
        at = first_chunk * plane_rows
        totals = []
        for q in range(PACK):
            total = None
            for dx in range(TAPS):
                part = jnp.dot(
                    window[pl.ds(pl.multiple_of(at + dx * blocks, blocks), size), q * depth:(q + 1) * depth],
                    taps[(dx * PACK + q) * depth:(dx * PACK + q + 1) * depth, :],
                    preferred_element_type=f32)
                total = part if total is None else total + part
            totals.append(total)
        squares = sum(total * total for total in totals)
        coarse = squares.astype(bf16)
        fine = (squares - coarse.astype(f32)).astype(bf16)
        mean = (jnp.dot(coarse, ones, preferred_element_type=f32)
                + jnp.dot(fine, ones, preferred_element_type=f32)) * (1.0 / channels)
        scale = lax.rsqrt(mean + EPSILON)
        gain = gain_ref[...].astype(f32)[layer:layer + 1] * 0.5
        low = is_low(size)
        for h in range(2):
            pair = gain[:, h * half:(h + 1) * half]
            other = swap(jnp.broadcast_to(pair, (8, half)))[0:1]
            low_row = is_low(1)
            even = jnp.where(low_row, pair, other)
            odd = jnp.where(low_row, other, pair)
            for v in range(2):
                lanes = slice(v * half, (v + 1) * half)
                a = totals[2 * h][:, lanes] * scale[:, lanes] * even
                b = totals[2 * h + 1][:, lanes] * scale[:, lanes] * odd
                for j, value in ((2 * v, jnp.where(low, a, swap(b))), (2 * v + 1, jnp.where(low, swap(a), b))):
                    value = value.astype(bf16)
                    for c in range(count):
                        to = pl.multiple_of((first_chunk + c) * rows + j * plane_rows, plane_rows)
                        normed[pl.ds(to, plane_rows), h * half:(h + 1) * half] = (
                            value[c * plane_rows:(c + 1) * plane_rows])

    def mix(layer, chunk):
        here = pl.ds(pl.multiple_of(chunk * rows, rows), rows)
        h = jnp.dot(normed[here, :], expand[layer * channels:(layer + 1) * channels, :],
                    preferred_element_type=f32).astype(bf16)
        hidden = h + h * jnp.tanh(h)
        out = jnp.dot(hidden, down[layer * hid:(layer + 1) * hid, :], preferred_element_type=f32)
        mixed[layer, here, :] = out.astype(bf16)

    def copy(layer, side, chunk):
        at = pl.multiple_of(chunk * rows, rows)
        landing = lower if side == 0 else upper
        d = DILATIONS[layer]
        return pltpu.make_async_remote_copy(
            src_ref=mixed.at[layer, pl.ds(at, rows), :],
            dst_ref=landing.at[layer, pl.ds(at, rows), :],
            send_sem=send_sem.at[layer, side, chunk],
            recv_sem=recv_sem.at[layer, side, chunk],
            device_id={"slab": me + (d if side == 0 else -d)},
            device_id_type=pl.DeviceIdType.MESH)

    def send(layer, chunk):
        for side in (0, 1):
            d = DILATIONS[layer]

            @pl.when(inside(me + (d if side == 0 else -d)))
            def _():
                copy(layer, side, chunk).start()

    def receive(layer, chunk):
        for side in (0, 1):
            d = DILATIONS[layer]

            @pl.when(inside(me - (d if side == 0 else -d)))
            def _():
                copy(layer, side, chunk).wait_recv()

    def combine(layer, at):
        coeffs = [depth_ref[k].astype(f32)[layer:layer + 1] for k in range(3)]
        here = pl.ds(at, rows)
        term = (coeffs[0] * lower[layer, here, :].astype(f32)
                + coeffs[1] * mixed[layer, here, :].astype(f32)
                + coeffs[2] * upper[layer, here, :].astype(f32))
        term = term.astype(bf16).astype(f32)
        return (cur[here, :].astype(f32) + term).astype(bf16).astype(f32)

    def mix_and_send(layer, first_chunk, count):
        def one(i, carry):
            mix(layer, i)
            send(layer, i)
            return carry
        lax.fori_loop(first_chunk, first_chunk + count, one, 0)

    loads[1].wait()

    def first_fill(i, carry):
        at = pl.multiple_of(i * rows, rows)
        value = vol[pl.ds(at, rows), :].astype(f32)
        for h in range(2):
            stage[h, pl.ds(at, rows), :] = value[:, h * half:(h + 1) * half]
        planes = [
            jnp.concatenate([stage[h, pl.ds(at + j, plane_rows, stride=PACK), :] for h in range(2)], axis=1)
            for j in range(PACK)]
        for j in range(PACK):
            cur[pl.ds(at + j * plane_rows, plane_rows), :] = planes[j].astype(bf16)
        fill(i, planes)
        return carry
    lax.fori_loop(0, CONV_CHUNKS + 1, first_fill, 0)
    loads[0].wait()
    build_taps(0)
    conv(0, 0, CONV_CHUNKS)
    loads[2].wait()
    loads[3].wait()
    pl.semaphore_wait(barrier, sum(inside(other).astype(jnp.int32) for _, _, other in reach))
    mix_and_send(0, 0, CONV_CHUNKS)
    lax.fori_loop(CONV_CHUNKS + 1, chunks, first_fill, 0)
    conv(0, CONV_CHUNKS, chunks - CONV_CHUNKS)
    mix_and_send(0, CONV_CHUNKS, chunks - CONV_CHUNKS)

    build_taps(1)

    def refill(i, carry):
        receive(0, i)
        at = pl.multiple_of(i * rows, rows)
        value = combine(0, at)
        cur[pl.ds(at, rows), :] = value.astype(bf16)
        fill(i, [value[j * plane_rows:(j + 1) * plane_rows] for j in range(PACK)])
        return carry

    lax.fori_loop(0, 1, refill, 0)

    def step(k, carry):
        start = k * CONV_CHUNKS
        lax.fori_loop(start + 1, jnp.minimum(start + 1 + CONV_CHUNKS, chunks), refill, 0)
        conv(1, start, CONV_CHUNKS)
        mix_and_send(1, start, CONV_CHUNKS)
        return carry
    lax.fori_loop(0, chunks // CONV_CHUNKS, step, 0)

    def store(i):
        at = pl.multiple_of(i * rows, rows)
        return pltpu.make_async_copy(result.at[pl.ds(at, rows), :], out_hbm.at[pl.ds(at, rows), :], out_sem.at[i])

    def last(i, carry):
        receive(1, i)
        at = pl.multiple_of(i * rows, rows)
        value = combine(1, at)
        for h in range(2):
            for j in range(PACK):
                stage[h, pl.ds(at + j, plane_rows, stride=PACK), :] = (
                    value[j * plane_rows:(j + 1) * plane_rows, h * half:(h + 1) * half])
            result[pl.ds(at, rows), h * half:(h + 1) * half] = stage[h, pl.ds(at, rows), :].astype(bf16)
        store(i).start()
        return carry
    lax.fori_loop(0, chunks, last, 0)

    def drain(i, carry):
        store(i).wait()
        for layer, side, other in reach:
            @pl.when(inside(other))
            def _():
                copy(layer, side, i).wait_send()
        return carry
    lax.fori_loop(0, chunks, drain, 0)


def shards(devices, volume, plane_weight, norm_gain, expand_weight, down_weight, depth_weight):
    slab_depth, extent_x, extent_y, channels = volume.shape
    layers, _, _, group, _ = plane_weight.shape
    hid = expand_weight.shape[2]
    cells = extent_x * extent_y
    chunks = extent_x // CHUNK_X
    bf16 = jnp.bfloat16
    whole = pl.BlockSpec(memory_space=pltpu.VMEM)
    far = pl.BlockSpec(memory_space=pl.ANY)
    out = pl.pallas_call(
        functools.partial(kernel, devices, extent_x, extent_y),
        out_shape=jax.ShapeDtypeStruct((cells, channels), bf16),
        in_specs=[far, far, whole, far, far, whole],
        out_specs=pl.BlockSpec(memory_space=pl.ANY),
        scratch_shapes=[
            pltpu.VMEM((cells, channels), bf16),
            pltpu.VMEM((2, cells, channels // 2), jnp.float32),
            pltpu.VMEM((cells, channels), bf16),
            pltpu.VMEM((layers * TAPS * TAPS * group, channels), bf16),
            pltpu.VMEM((layers * channels, hid), bf16),
            pltpu.VMEM((layers * hid, channels), bf16),
            pltpu.VMEM((TAPS * PACK * 2 * channels, channels), bf16),
            pltpu.VMEM(((extent_x + 4) * extent_y // PACK, PACK * 2 * channels), bf16),
            pltpu.VMEM((cells, channels), bf16),
            pltpu.VMEM((layers, cells, channels), bf16),
            pltpu.VMEM((layers, cells, channels), bf16),
            pltpu.VMEM((layers, cells, channels), bf16),
            pltpu.VMEM((cells, channels), bf16),
            pltpu.SemaphoreType.DMA((4,)),
            pltpu.SemaphoreType.DMA((layers, 2, chunks)),
            pltpu.SemaphoreType.DMA((layers, 2, chunks)),
            pltpu.SemaphoreType.DMA((chunks,)),
        ],
        compiler_params=pltpu.CompilerParams(
            collective_id=0, has_side_effects=True, vmem_limit_bytes=54 * 1024 * 1024),
        cost_estimate=pl.CostEstimate(flops=9 * 10**9, bytes_accessed=5 * 10**6, transcendentals=2 * 10**6),
    )(
        volume.reshape(cells, channels),
        plane_weight.reshape(layers * TAPS * TAPS * group, channels),
        norm_gain,
        expand_weight.reshape(layers * channels, hid),
        down_weight.reshape(layers * hid, channels),
        depth_weight.transpose(1, 0, 2),
    )
    return out.reshape(volume.shape)


def solution(mesh):
    placed = (P(("parts", "slab"), None, None, None), P(), P(), P(), P(), P())
    return jax.shard_map(
        functools.partial(shards, mesh.shape["slab"]),
        mesh=mesh,
        in_specs=placed,
        out_specs=P(("parts", "slab"), None, None, None),
        check_vma=False,
    )
```

```python
import functools

import jax
import jax.numpy as jnp
from jax import lax
from jax.experimental import pallas as pl
from jax.experimental.pallas import tpu as pltpu
from jax.sharding import PartitionSpec as P

DILATIONS = (1, 4)
TAPS = 5
EPSILON = 1e-06
CHUNK_X = 4
PACK = 4
CONV_CHUNKS = 1


def kernel(devices, extent_x, extent_y, vol_hbm, plane_hbm, gain_ref, expand_hbm, down_hbm, depth_ref, out_hbm,
           vol, stage, cur, plane, expand, down, taps, window, normed, mixed, lower, upper, result,
           load_sem, send_sem, recv_sem, out_sem):
    me = lax.axis_index("slab")
    channels = cur.shape[1]
    group = plane.shape[0] // (2 * TAPS * TAPS)
    blocks = extent_y // PACK
    plane_rows = CHUNK_X * blocks
    rows = PACK * plane_rows
    chunks = extent_x // CHUNK_X
    halo = 2 * blocks
    hid = expand.shape[1]
    half = channels // 2
    quarter = channels // PACK
    depth = 2 * channels
    bf16, f32 = jnp.bfloat16, jnp.float32

    loads = [
        pltpu.make_async_copy(src, dst, load_sem.at[k])
        for k, (src, dst) in enumerate(
            ((plane_hbm, plane), (vol_hbm, vol), (expand_hbm, expand), (down_hbm, down)))
    ]
    for load in loads:
        load.start()

    reach = [(layer, side, me + (d if side == 0 else -d))
             for layer, d in enumerate(DILATIONS) for side in (0, 1)]

    def inside(other):
        return jnp.logical_and(other >= 0, other < devices)

    barrier = pltpu.get_barrier_semaphore()
    for _, _, other in reach:
        @pl.when(inside(other))
        def _():
            pl.semaphore_signal(barrier, inc=1, device_id={"slab": other}, device_id_type=pl.DeviceIdType.MESH)

    edge = jnp.zeros((halo, PACK * depth), bf16)
    window[:halo, :] = edge
    window[halo + extent_x * blocks:, :] = edge

    for layer, side, other in reach:
        source = me - (other - me)
        landing = lower if side == 0 else upper

        @pl.when(jnp.logical_not(inside(source)))
        def _():
            landing[layer] = jnp.zeros(landing.shape[1:], bf16)

    def is_low(count):
        return lax.broadcasted_iota(jnp.int32, (count, half), 1) < quarter

    def swap(value):
        return pltpu.roll(value, quarter, 1)

    lane_group = lax.broadcasted_iota(jnp.int32, (group, half), 1) % quarter // group
    group_mask = [jnp.where(lane_group == g, 1.0, 0.0).astype(bf16) for g in range(quarter // group)]

    def clear(t, carry):
        for v, start in ((0, 6 * quarter), (1, 0)):
            taps[pl.ds(pl.multiple_of(t * depth + start, 2 * quarter), 2 * quarter), v * half:(v + 1) * half] = (
                jnp.zeros((2 * quarter, half), bf16))
        return carry
    lax.fori_loop(0, TAPS * PACK, clear, 0)

    def build_taps(layer):
        def one(dx, carry):
            base = (layer * TAPS + dx) * TAPS * group
            for h in range(2):
                straight = [
                    plane[pl.ds(pl.multiple_of(base + dy * group, group), group), h * half:(h + 1) * half].astype(f32)
                    for dy in range(TAPS)]
                swapped = [swap(value) for value in straight]
                zero = jnp.zeros((group, half), f32)
                for odd in range(2):
                    left, right = (swapped, straight) if odd else (straight, swapped)
                    at = pl.multiple_of((dx * PACK + 2 * h + odd) * depth, depth)
                    for k in range(TAPS + 1):
                        pair = jnp.where(
                            is_low(group), left[k] if k < TAPS else zero, right[k - 1] if k > 0 else zero).astype(bf16)
                        for g, only in enumerate(group_mask):
                            tile = pair * only
                            for v in range(2):
                                taps[pl.ds(at + (k + 2 * v) * quarter + g * group, group),
                                     v * half:(v + 1) * half] = tile
            return carry
        lax.fori_loop(0, TAPS, one, 0)

    def fill(chunk, planes):
        block = lax.broadcasted_iota(jnp.int32, (plane_rows, channels), 0) % blocks

        def before(value):
            return jnp.where(block == 0, 0.0, pltpu.roll(value, 1, 0))

        def after(value):
            return jnp.where(block == blocks - 1, 0.0, pltpu.roll(value, plane_rows - 1, 0))

        y = [before(planes[2]), before(planes[3]), *planes, after(planes[0]), after(planes[1])]
        here = pl.ds(pl.multiple_of(chunk * plane_rows + halo, halo), plane_rows)
        low = is_low(plane_rows)
        for k in range(0, 2 * PACK, 2):
            for h in range(2):
                a = y[k][:, h * half:(h + 1) * half]
                b = y[k + 1][:, h * half:(h + 1) * half]
                at = 2 * h * depth + k * quarter
                window[here, at:at + half] = jnp.where(low, a, swap(b)).astype(bf16)
                window[here, at + depth:at + depth + half] = jnp.where(low, swap(a), b).astype(bf16)

    ones = jnp.where(
        lax.broadcasted_iota(jnp.int32, (channels, channels), 0) // quarter
        == lax.broadcasted_iota(jnp.int32, (channels, channels), 1) // quarter, 1.0, 0.0).astype(bf16)

    def conv(layer, first_chunk, count):
        size = count * plane_rows
        at = first_chunk * plane_rows
        totals = []
        for q in range(PACK):
            total = None
            for dx in range(TAPS):
                part = jnp.dot(
                    window[pl.ds(pl.multiple_of(at + dx * blocks, blocks), size), q * depth:(q + 1) * depth],
                    taps[(dx * PACK + q) * depth:(dx * PACK + q + 1) * depth, :],
                    preferred_element_type=f32)
                total = part if total is None else total + part
            totals.append(total)
        squares = sum(total * total for total in totals)
        coarse = squares.astype(bf16)
        fine = (squares - coarse.astype(f32)).astype(bf16)
        mean = (jnp.dot(coarse, ones, preferred_element_type=f32)
                + jnp.dot(fine, ones, preferred_element_type=f32)) * (1.0 / channels)
        scale = lax.rsqrt(mean + EPSILON)
        gain = gain_ref[...].astype(f32)[layer:layer + 1] * 0.5
        low = is_low(size)
        for h in range(2):
            pair = gain[:, h * half:(h + 1) * half]
            other = swap(jnp.broadcast_to(pair, (8, half)))[0:1]
            low_row = is_low(1)
            even = jnp.where(low_row, pair, other)
            odd = jnp.where(low_row, other, pair)
            for v in range(2):
                lanes = slice(v * half, (v + 1) * half)
                a = totals[2 * h][:, lanes] * scale[:, lanes] * even
                b = totals[2 * h + 1][:, lanes] * scale[:, lanes] * odd
                for j, value in ((2 * v, jnp.where(low, a, swap(b))), (2 * v + 1, jnp.where(low, swap(a), b))):
                    value = value.astype(bf16)
                    for c in range(count):
                        to = pl.multiple_of((first_chunk + c) * rows + j * plane_rows, plane_rows)
                        normed[pl.ds(to, plane_rows), h * half:(h + 1) * half] = (
                            value[c * plane_rows:(c + 1) * plane_rows])

    def mix(layer, chunk):
        here = pl.ds(pl.multiple_of(chunk * rows, rows), rows)
        h = jnp.dot(normed[here, :], expand[layer * channels:(layer + 1) * channels, :],
                    preferred_element_type=f32).astype(bf16)
        hidden = h + h * jnp.tanh(h)
        out = jnp.dot(hidden, down[layer * hid:(layer + 1) * hid, :], preferred_element_type=f32)
        mixed[layer, here, :] = out.astype(bf16)

    def copy(layer, side, chunk):
        at = pl.multiple_of(chunk * rows, rows)
        landing = lower if side == 0 else upper
        d = DILATIONS[layer]
        return pltpu.make_async_remote_copy(
            src_ref=mixed.at[layer, pl.ds(at, rows), :],
            dst_ref=landing.at[layer, pl.ds(at, rows), :],
            send_sem=send_sem.at[layer, side, chunk],
            recv_sem=recv_sem.at[layer, side, chunk],
            device_id={"slab": me + (d if side == 0 else -d)},
            device_id_type=pl.DeviceIdType.MESH)

    def send(layer, chunk):
        for side in (0, 1):
            d = DILATIONS[layer]

            @pl.when(inside(me + (d if side == 0 else -d)))
            def _():
                copy(layer, side, chunk).start()

    def receive(layer, chunk):
        for side in (0, 1):
            d = DILATIONS[layer]

            @pl.when(inside(me - (d if side == 0 else -d)))
            def _():
                copy(layer, side, chunk).wait_recv()

    def combine(layer, at):
        coeffs = [depth_ref[k].astype(f32)[layer:layer + 1] for k in range(3)]
        here = pl.ds(at, rows)
        term = (coeffs[0] * lower[layer, here, :].astype(f32)
                + coeffs[1] * mixed[layer, here, :].astype(f32)
                + coeffs[2] * upper[layer, here, :].astype(f32))
        term = term.astype(bf16).astype(f32)
        return (cur[here, :].astype(f32) + term).astype(bf16).astype(f32)

    def mix_and_send(layer, first_chunk, count):
        def one(i, carry):
            mix(layer, i)
            send(layer, i)
            return carry
        lax.fori_loop(first_chunk, first_chunk + count, one, 0)

    loads[1].wait()

    def first_fill(i, carry):
        at = pl.multiple_of(i * rows, rows)
        value = vol[pl.ds(at, rows), :].astype(f32)
        for h in range(2):
            stage[h, pl.ds(at, rows), :] = value[:, h * half:(h + 1) * half]
        planes = [
            jnp.concatenate([stage[h, pl.ds(at + j, plane_rows, stride=PACK), :] for h in range(2)], axis=1)
            for j in range(PACK)]
        for j in range(PACK):
            cur[pl.ds(at + j * plane_rows, plane_rows), :] = planes[j].astype(bf16)
        fill(i, planes)
        return carry
    lax.fori_loop(0, CONV_CHUNKS + 1, first_fill, 0, unroll=True)
    loads[0].wait()
    build_taps(0)
    conv(0, 0, CONV_CHUNKS)
    loads[2].wait()
    loads[3].wait()
    pl.semaphore_wait(barrier, sum(inside(other).astype(jnp.int32) for _, _, other in reach))
    mix_and_send(0, 0, CONV_CHUNKS)
    lax.fori_loop(CONV_CHUNKS + 1, chunks, first_fill, 0, unroll=True)
    conv(0, CONV_CHUNKS, chunks - CONV_CHUNKS)
    mix_and_send(0, CONV_CHUNKS, chunks - CONV_CHUNKS)

    build_taps(1)

    def refill(i, carry):
        receive(0, i)
        at = pl.multiple_of(i * rows, rows)
        value = combine(0, at)
        cur[pl.ds(at, rows), :] = value.astype(bf16)
        fill(i, [value[j * plane_rows:(j + 1) * plane_rows] for j in range(PACK)])
        return carry

    lax.fori_loop(0, 1, refill, 0)

    def step(k, carry):
        start = k * CONV_CHUNKS
        lax.fori_loop(start + 1, jnp.minimum(start + 1 + CONV_CHUNKS, chunks), refill, 0)
        conv(1, start, CONV_CHUNKS)
        mix_and_send(1, start, CONV_CHUNKS)
        return carry
    lax.fori_loop(0, chunks // CONV_CHUNKS, step, 0)

    def store(i):
        at = pl.multiple_of(i * rows, rows)
        return pltpu.make_async_copy(result.at[pl.ds(at, rows), :], out_hbm.at[pl.ds(at, rows), :], out_sem.at[i])

    def last(i, carry):
        receive(1, i)
        at = pl.multiple_of(i * rows, rows)
        value = combine(1, at)
        for h in range(2):
            for j in range(PACK):
                stage[h, pl.ds(at + j, plane_rows, stride=PACK), :] = (
                    value[j * plane_rows:(j + 1) * plane_rows, h * half:(h + 1) * half])
            result[pl.ds(at, rows), h * half:(h + 1) * half] = stage[h, pl.ds(at, rows), :].astype(bf16)
        store(i).start()
        return carry
    lax.fori_loop(0, chunks, last, 0)

    def drain(i, carry):
        store(i).wait()
        for layer, side, other in reach:
            @pl.when(inside(other))
            def _():
                copy(layer, side, i).wait_send()
        return carry
    lax.fori_loop(0, chunks, drain, 0)


def shards(devices, volume, plane_weight, norm_gain, expand_weight, down_weight, depth_weight):
    slab_depth, extent_x, extent_y, channels = volume.shape
    layers, _, _, group, _ = plane_weight.shape
    hid = expand_weight.shape[2]
    cells = extent_x * extent_y
    chunks = extent_x // CHUNK_X
    bf16 = jnp.bfloat16
    whole = pl.BlockSpec(memory_space=pltpu.VMEM)
    far = pl.BlockSpec(memory_space=pl.ANY)
    out = pl.pallas_call(
        functools.partial(kernel, devices, extent_x, extent_y),
        out_shape=jax.ShapeDtypeStruct((cells, channels), bf16),
        in_specs=[far, far, whole, far, far, whole],
        out_specs=pl.BlockSpec(memory_space=pl.ANY),
        scratch_shapes=[
            pltpu.VMEM((cells, channels), bf16),
            pltpu.VMEM((2, cells, channels // 2), jnp.float32),
            pltpu.VMEM((cells, channels), bf16),
            pltpu.VMEM((layers * TAPS * TAPS * group, channels), bf16),
            pltpu.VMEM((layers * channels, hid), bf16),
            pltpu.VMEM((layers * hid, channels), bf16),
            pltpu.VMEM((TAPS * PACK * 2 * channels, channels), bf16),
            pltpu.VMEM(((extent_x + 4) * extent_y // PACK, PACK * 2 * channels), bf16),
            pltpu.VMEM((cells, channels), bf16),
            pltpu.VMEM((layers, cells, channels), bf16),
            pltpu.VMEM((layers, cells, channels), bf16),
            pltpu.VMEM((layers, cells, channels), bf16),
            pltpu.VMEM((cells, channels), bf16),
            pltpu.SemaphoreType.DMA((4,)),
            pltpu.SemaphoreType.DMA((layers, 2, chunks)),
            pltpu.SemaphoreType.DMA((layers, 2, chunks)),
            pltpu.SemaphoreType.DMA((chunks,)),
        ],
        compiler_params=pltpu.CompilerParams(
            collective_id=0, has_side_effects=True, vmem_limit_bytes=54 * 1024 * 1024),
        cost_estimate=pl.CostEstimate(flops=9 * 10**9, bytes_accessed=5 * 10**6, transcendentals=2 * 10**6),
    )(
        volume.reshape(cells, channels),
        plane_weight.reshape(layers * TAPS * TAPS * group, channels),
        norm_gain,
        expand_weight.reshape(layers * channels, hid),
        down_weight.reshape(layers * hid, channels),
        depth_weight.transpose(1, 0, 2),
    )
    return out.reshape(volume.shape)


def solution(mesh):
    placed = (P(("parts", "slab"), None, None, None), P(), P(), P(), P(), P())
    return jax.shard_map(
        functools.partial(shards, mesh.shape["slab"]),
        mesh=mesh,
        in_specs=placed,
        out_specs=P(("parts", "slab"), None, None, None),
        check_vma=False,
    )
```

```python
import functools

import jax
import jax.numpy as jnp
from jax import lax
from jax.experimental import pallas as pl
from jax.experimental.pallas import tpu as pltpu
from jax.sharding import PartitionSpec as P

DILATIONS = (1, 4)
TAPS = 5
EPSILON = 1e-06
CHUNK_X = 4


def kernel(devices, extent_x, extent_y, vol_hbm, plane_hbm, gain_ref, expand_hbm, down_hbm, depth_ref, base_hbm, term_hbm,
           cur, plane, expand, down, mask, taps, window, mixed, lower, upper, result,
           load_sem, send_sem, recv_sem, out_sem):
    me = lax.axis_index("slab")
    channels = cur.shape[1]
    group = plane.shape[0] // (2 * TAPS * TAPS)
    rows = CHUNK_X * extent_y
    chunks = extent_x // CHUNK_X
    halo = 2 * extent_y
    hid = expand.shape[1]

    loads = [
        pltpu.make_async_copy(src, dst, load_sem.at[k])
        for k, (src, dst) in enumerate(
            ((plane_hbm, plane), (vol_hbm, cur), (expand_hbm, expand), (down_hbm, down)))
    ]
    for load in loads:
        load.start()

    reach = [(layer, side, me + (d if side == 0 else -d))
             for layer, d in enumerate(DILATIONS) for side in (0, 1)]

    def inside(other):
        return jnp.logical_and(other >= 0, other < devices)

    barrier = pltpu.get_barrier_semaphore()
    for _, _, other in reach:
        @pl.when(inside(other))
        def _():
            pl.semaphore_signal(barrier, inc=1, device_id={"slab": other}, device_id_type=pl.DeviceIdType.MESH)

    row_group = lax.broadcasted_iota(jnp.int32, (channels, channels), 0) // group
    column_group = lax.broadcasted_iota(jnp.int32, (channels, channels), 1) // group
    mask[...] = jnp.where(row_group == column_group, 1.0, 0.0).astype(jnp.bfloat16)
    edge = jnp.zeros((halo, TAPS * channels), jnp.bfloat16)
    window[:halo, :] = edge
    window[halo + extent_x * extent_y:, :] = edge

    for layer, side, other in reach:
        source = me - (other - me)
        landing = lower if side == 0 else upper

        @pl.when(jnp.logical_not(inside(source)))
        def _():
            landing[layer] = jnp.zeros(landing.shape[1:], jnp.bfloat16)

    def build_taps(layer):
        def one(t, carry):
            tap = plane[pl.ds(pl.multiple_of((layer * TAPS * TAPS + t) * group, group), group), :]
            tiled = jnp.concatenate([tap] * (channels // group), axis=0)
            taps[pl.ds(pl.multiple_of(t * channels, channels), channels), :] = tiled * mask[...]
            return carry
        lax.fori_loop(0, TAPS * TAPS, one, 0)

    def fill(at, value):
        y = lax.broadcasted_iota(jnp.int32, (rows, channels), 0) % extent_y
        for dy in range(TAPS):
            shift = dy - 2
            if shift == 0:
                moved = value
            else:
                moved = pltpu.roll(value, (-shift) % rows, 0)
                inside_y = jnp.logical_and(y + shift >= 0, y + shift < extent_y)
                moved = jnp.where(inside_y, moved, 0.0)
            window[pl.ds(at + halo, rows), dy * channels:(dy + 1) * channels] = moved.astype(jnp.bfloat16)

    def mix(layer, at):
        total = None
        for dx in range(TAPS):
            part = jnp.dot(
                window[pl.ds(pl.multiple_of(at + dx * extent_y, extent_y), rows), :],
                taps[dx * TAPS * channels:(dx + 1) * TAPS * channels, :],
                preferred_element_type=jnp.float32)
            total = part if total is None else total + part
        scale = lax.rsqrt(jnp.mean(total * total, axis=-1, keepdims=True) + EPSILON)
        gain = gain_ref[...].astype(jnp.float32)[layer:layer + 1] * 0.5
        half = (total * scale * gain).astype(jnp.bfloat16)
        h = jnp.dot(half, expand[layer * channels:(layer + 1) * channels, :], preferred_element_type=jnp.float32)
        hidden = (h + h * jnp.tanh(h)).astype(jnp.bfloat16)
        out = jnp.dot(hidden, down[layer * hid:(layer + 1) * hid, :], preferred_element_type=jnp.float32)
        mixed[layer, pl.ds(at, rows), :] = out.astype(jnp.bfloat16)

    def copy(layer, side, chunk):
        at = pl.multiple_of(chunk * rows, rows)
        landing = lower if side == 0 else upper
        d = DILATIONS[layer]
        return pltpu.make_async_remote_copy(
            src_ref=mixed.at[layer, pl.ds(at, rows), :],
            dst_ref=landing.at[layer, pl.ds(at, rows), :],
            send_sem=send_sem.at[layer, side, chunk],
            recv_sem=recv_sem.at[layer, side, chunk],
            device_id={"slab": me + (d if side == 0 else -d)},
            device_id_type=pl.DeviceIdType.MESH)

    def send(layer, chunk):
        for side in (0, 1):
            d = DILATIONS[layer]

            @pl.when(inside(me + (d if side == 0 else -d)))
            def _():
                copy(layer, side, chunk).start()

    def receive(layer, chunk):
        for side in (0, 1):
            d = DILATIONS[layer]

            @pl.when(inside(me - (d if side == 0 else -d)))
            def _():
                copy(layer, side, chunk).wait_recv()

    def combine(layer, at):
        coeffs = [depth_ref[k].astype(jnp.float32)[layer:layer + 1] for k in range(3)]
        here = pl.ds(at, rows)
        term = (coeffs[0] * lower[layer, here, :].astype(jnp.float32)
                + coeffs[1] * mixed[layer, here, :].astype(jnp.float32)
                + coeffs[2] * upper[layer, here, :].astype(jnp.float32))
        return term.astype(jnp.bfloat16)

    loads[0].wait()
    build_taps(0)
    loads[1].wait()

    def first_fill(i, carry):
        at = pl.multiple_of(i * rows, rows)
        fill(at, cur[pl.ds(at, rows), :].astype(jnp.float32))
        return carry
    lax.fori_loop(0, chunks, first_fill, 0)
    loads[2].wait()
    loads[3].wait()
    pl.semaphore_wait(barrier, sum(inside(other).astype(jnp.int32) for _, _, other in reach))

    def first(i, carry):
        mix(0, pl.multiple_of(i * rows, rows))
        send(0, i)
        return carry
    lax.fori_loop(0, chunks, first, 0)

    build_taps(1)

    def second(i, carry):
        @pl.when(i < chunks)
        def _():
            receive(0, i)
            at = pl.multiple_of(i * rows, rows)
            value = (cur[pl.ds(at, rows), :].astype(jnp.float32) + combine(0, at).astype(jnp.float32)).astype(jnp.bfloat16)
            cur[pl.ds(at, rows), :] = value
            fill(at, value.astype(jnp.float32))

        @pl.when(i >= 1)
        def _():
            mix(1, pl.multiple_of((i - 1) * rows, rows))
            send(1, i - 1)
        return carry
    lax.fori_loop(0, chunks + 1, second, 0)

    def store(i):
        at = pl.multiple_of(i * rows, rows)
        return pltpu.make_async_copy(result.at[pl.ds(at, rows), :], term_hbm.at[pl.ds(at, rows), :], out_sem.at[i])

    base = pltpu.make_async_copy(cur, base_hbm, load_sem.at[0])
    base.start()

    def last(i, carry):
        receive(1, i)
        at = pl.multiple_of(i * rows, rows)
        result[pl.ds(at, rows), :] = combine(1, at)
        store(i).start()
        return carry
    lax.fori_loop(0, chunks, last, 0)

    def drain(i, carry):
        store(i).wait()
        for layer, side, other in reach:
            @pl.when(inside(other))
            def _():
                copy(layer, side, i).wait_send()
        return carry
    lax.fori_loop(0, chunks, drain, 0)
    base.wait()


def shards(devices, volume, plane_weight, norm_gain, expand_weight, down_weight, depth_weight):
    slab_depth, extent_x, extent_y, channels = volume.shape
    layers, _, _, group, _ = plane_weight.shape
    hid = expand_weight.shape[2]
    cells = extent_x * extent_y
    chunks = extent_x // CHUNK_X
    bf16 = jnp.bfloat16
    whole = pl.BlockSpec(memory_space=pltpu.VMEM)
    far = pl.BlockSpec(memory_space=pl.ANY)
    base, term = pl.pallas_call(
        functools.partial(kernel, devices, extent_x, extent_y),
        out_shape=[jax.ShapeDtypeStruct((cells, channels), bf16)] * 2,
        in_specs=[far, far, whole, far, far, whole],
        out_specs=[far, far],
        scratch_shapes=[
            pltpu.VMEM((cells, channels), bf16),
            pltpu.VMEM((layers * TAPS * TAPS * group, channels), bf16),
            pltpu.VMEM((layers * channels, hid), bf16),
            pltpu.VMEM((layers * hid, channels), bf16),
            pltpu.VMEM((channels, channels), bf16),
            pltpu.VMEM((TAPS * TAPS * channels, channels), bf16),
            pltpu.VMEM((cells + 4 * extent_y, TAPS * channels), bf16),
            pltpu.VMEM((layers, cells, channels), bf16),
            pltpu.VMEM((layers, cells, channels), bf16),
            pltpu.VMEM((layers, cells, channels), bf16),
            pltpu.VMEM((cells, channels), bf16),
            pltpu.SemaphoreType.DMA((4,)),
            pltpu.SemaphoreType.DMA((layers, 2, chunks)),
            pltpu.SemaphoreType.DMA((layers, 2, chunks)),
            pltpu.SemaphoreType.DMA((chunks,)),
        ],
        compiler_params=pltpu.CompilerParams(
            collective_id=0, has_side_effects=True, vmem_limit_bytes=54 * 1024 * 1024),
        cost_estimate=pl.CostEstimate(flops=9 * 10**9, bytes_accessed=5 * 10**6, transcendentals=2 * 10**6),
    )(
        volume.reshape(cells, channels),
        plane_weight.reshape(layers * TAPS * TAPS * group, channels),
        norm_gain,
        expand_weight.reshape(layers * channels, hid),
        down_weight.reshape(layers * hid, channels),
        depth_weight.transpose(1, 0, 2),
    )
    return (base.astype(jnp.float32) + term.astype(jnp.float32)).astype(bf16).reshape(volume.shape)


def solution(mesh):
    placed = (P(("parts", "slab"), None, None, None), P(), P(), P(), P(), P())
    return jax.shard_map(
        functools.partial(shards, mesh.shape["slab"]),
        mesh=mesh,
        in_specs=placed,
        out_specs=P(("parts", "slab"), None, None, None),
        check_vma=False,
    )
```
